32 devices in a mesh: row: 4 (over x, core), col: 4 (over z), depth: 2 (over y).
Axes of the slice: x: 2, y: 2, z: 4, core: 2. Of those that a mesh axis runs over, the one named last changes fastest.
Arguments:
- front_matrix: float32 [2, 8192, 8192], P('depth', 'row', 'col'), as said below
- block_mask: int32 [2, 64, 64], P('depth', 'row', 'col'), may hold values 0 or 1
- supernode_width: int32 [2, 3], P('depth'), may hold values from 128 to 256, as said below
Outputs:
- schur: float32 [2, 8192, 8192], P('depth', 'row', 'col')
- ancestor: float32 [4096, 4096], P('row', ('col', 'depth'))
The draws below stay inside these ranges and needn't reach their ends.
Inputs may be any that keep to these rules, and one draw needn't show every extreme that they name: `front_matrix`: restricted to its first 768 rows and columns, each front is row diagonally dominant: each diagonal entry is positive and at least 1.5 times the sum of the magnitudes of the other entries of its row among those columns. `supernode_width`: each entry is a multiple of 128; in each front one supernode has the full width 256.
All inputs are finite; a program needn't handle non-finite values. No bound on the sum of `block_mask` on one device may be relied on, other than what follows from the above.
Results may differ from the reference program's by a relative error of at most 0.0001.
Values sent between devices are 32-bit elements; how exact they have to be, the bound alone decides.
A program may use at most 128 MiB of HBM per device.

```python
import jax
import jax.numpy as jnp
from jax import lax

F = 8192
SN = 256
BLK = 128
NSN = 3
LAYERS = 2
PIV = 768


def draw_front_matrix(key, part):
    shape_all = (LAYERS, F, F)
    key_noise = jax.random.fold_in(key, 101)
    key_across = jax.random.fold_in(key, 202)
    key_down = jax.random.fold_in(key, 303)
    noise = jax.random.normal(key_noise, shape_all, jnp.float32)
    across = jax.random.normal(key_across, (LAYERS, 1, F), jnp.float32)
    down = jax.random.normal(key_down, (LAYERS, F, 1), jnp.float32)
    position = jnp.arange(F)
    in_pivot = position < PIV
    both_pivot = (in_pivot[:, None] & in_pivot[None, :])[None]
    band_part = (in_pivot[:, None] & ~in_pivot[None, :])[None]
    panel_part = (~in_pivot[:, None] & in_pivot[None, :])[None]
    coupled = jnp.abs(noise) + 0.5 * noise
    values = jnp.where(both_pivot, coupled, noise)
    values = jnp.where(band_part, 2.0 * (across + noise), values)
    values = jnp.where(panel_part, 2.0 * (down + noise), values)
    diagonal_pos = (position[:, None] == position[None, :])[None]
    offsum = jnp.sum(jnp.where(both_pivot & ~diagonal_pos, jnp.abs(values), 0.0), axis=-1)
    diagonal = 1.5 * offsum + 1.0
    values = jnp.where(diagonal_pos & both_pivot, diagonal[:, :, None], values)
    return values.astype(jnp.float32)


def draw_supernode_width(key, part):
    key_count = jax.random.fold_in(key, 11)
    key_full = jax.random.fold_in(key, 23)
    most = SN // BLK
    counts = jax.random.randint(key_count, (LAYERS, NSN), 1, most + 1)
    full_slot = jax.random.randint(key_full, (LAYERS,), 0, NSN)
    counts = jnp.where(jnp.arange(NSN)[None, :] == full_slot[:, None], most, counts)
    return (counts * BLK).astype(jnp.int32)


def plant(array, own_key, low, top_value):
    spot = [jax.random.randint(jax.random.fold_in(own_key, axis), (), 0, length) for axis, length in enumerate(array.shape)]
    main_axis = array.shape.index(max(array.shape))
    beside = spot[:main_axis] + [(spot[main_axis] + 1) % array.shape[main_axis]] + spot[main_axis + 1:]
    return array.at[tuple(spot)].set(low).at[tuple(beside)].set(top_value)


def setup_inputs(seed: int = 0) -> dict:
    key_list = jax.random.split(jax.random.key(seed), 4)
    return {
        "front_matrix": draw_front_matrix(jax.random.fold_in(key_list[3], 71), 0),
        "block_mask": plant((jax.random.randint(key_list[1], (LAYERS, F // BLK, F // BLK), 0, 2) < 1).astype(jnp.int32), jax.random.fold_in(key_list[1], 1), 0, 1),
        "supernode_width": draw_supernode_width(jax.random.fold_in(key_list[3], 71), 0),
    }


def eliminate(matrix, widths):
    order = matrix.shape[0]
    position = jnp.arange(order)
    finished = jnp.zeros((order,), jnp.float32)
    for supernode in range(NSN):
        pivot_start = supernode * SN
        pivots = (jnp.arange(SN) < widths[supernode]).astype(jnp.float32)
        column_panel = matrix[:, pivot_start:pivot_start + SN] * pivots[None, :]
        row_band = matrix[pivot_start:pivot_start + SN, :] * pivots[:, None]
        pivot_block = matrix[pivot_start:pivot_start + SN, pivot_start:pivot_start + SN] * pivots[:, None] * pivots[None, :] + jnp.diag(1.0 - pivots)
        solved = jnp.linalg.solve(pivot_block, row_band)
        update = jnp.dot(column_panel, solved, precision=lax.Precision.HIGHEST)
        chosen = ((position >= pivot_start) & (position < pivot_start + widths[supernode])).astype(jnp.float32)
        live_set = 1.0 - finished - chosen
        matrix = matrix - live_set[:, None] * live_set[None, :] * update
        finished = finished + chosen
    return matrix

def reference(front_matrix, block_mask, supernode_width):
    blocks_per = F // BLK
    block_ids = jnp.arange(blocks_per)
    outputs = []
    ancestor = None
    for layer_index in range(LAYERS):
        kept_blocks = ((block_mask[layer_index] != 0) | (block_ids[:, None] == block_ids[None, :])).astype(jnp.float32)
        matrix = (front_matrix[layer_index].reshape(blocks_per, BLK, blocks_per, BLK) * kept_blocks[:, None, :, None]).reshape(F, F)
        matrix = eliminate(matrix, supernode_width[layer_index])
        outputs.append(matrix)
        quarter = matrix.reshape(blocks_per, BLK, blocks_per, BLK)[1::2, :, 1::2, :].reshape(F // 2, F // 2)
        if layer_index == 0:
            ancestor = quarter
        else:
            ancestor = ancestor + quarter
    return (jnp.stack(outputs), ancestor)
```

```python
import functools

import jax
import jax.numpy as jnp
from jax import lax
from jax.experimental import pallas as pl
from jax.experimental.pallas import tpu as pltpu
from jax.sharding import PartitionSpec as P

SN = 256
BLK = 128
NSN = 3
PIV = SN * NSN
HIGHEST = lax.Precision.HIGHEST
MESH = pl.DeviceIdType.MESH


def from_root(value, axis, source):
    kept = jnp.where(lax.axis_index(axis) == source, value, 0).astype(value.dtype)
    return lax.psum(kept, axis)


def expand_blocks(matrix, kept_blocks):
    height, breadth = matrix.shape
    shaped = matrix.reshape(height // BLK, BLK, breadth // BLK, BLK)
    return jnp.where(kept_blocks[:, None, :, None], shaped, 0.0).reshape(height, breadth)


def masked_kernel(kept, a_ref, out_ref):
    step = pl.program_id(0)
    rows, cols = a_ref.shape
    for b in range(rows // BLK):
        for j in range(cols // BLK):
            keep = kept[step * (rows // BLK) + b, j] != 0
            here = (slice(b * BLK, (b + 1) * BLK), slice(j * BLK, (j + 1) * BLK))
            out_ref[here] = jnp.where(keep, a_ref[here], 0.0)


def masked_window(kept, matrix, rows, cols):
    tile = 2 * BLK
    return pl.pallas_call(
        masked_kernel,
        grid=(rows // tile,),
        out_shape=jax.ShapeDtypeStruct((rows, cols), jnp.float32),
        in_specs=[
            pl.BlockSpec(memory_space=pltpu.SMEM),
            pl.BlockSpec((tile, cols), lambda i: (i, 0)),
        ],
        out_specs=pl.BlockSpec((tile, cols), lambda i: (i, 0)),
        compiler_params=pltpu.CompilerParams(vmem_limit_bytes=32 * 1024 * 1024),
        name="masked_window",
    )(kept, matrix)


def spread_kernel(n_row, n_col, strip_in, band_in, strip, band, pivot, *sems):
    (strip_send, strip_recv, band_send, band_pair, band_recv, piv_send, piv_pair, piv_recv) = sems
    del strip_in, band_in
    row = lax.axis_index("row")
    col = lax.axis_index("col")
    even = lax.rem(row, 2) == 0
    has_next = even & (row + 2 < n_row)
    height = strip.shape[0]
    strip_rows = BLK
    band_rows = BLK // 2
    piv_rows = BLK

    barrier = pltpu.get_barrier_semaphore()

    def greet(when, target):
        @pl.when(when)
        def _():
            pl.semaphore_signal(barrier, inc=1, device_id=target, device_id_type=MESH)

    greet(col > 0, {"col": col - 1})
    greet(col < n_col - 1, {"col": col + 1})
    greet(even, {"row": row + 1})
    greet(jnp.logical_not(even), {"row": row - 1})
    greet(has_next, {"row": row + 2})
    greet(even & (row >= 2), {"row": row - 2})

    peers = (col > 0).astype(jnp.int32) + (col < n_col - 1).astype(jnp.int32) + 1
    peers += has_next.astype(jnp.int32) + (even & (row >= 2)).astype(jnp.int32)
    pl.semaphore_wait(barrier, peers)

    def remote(src, dst, send, recv, target):
        return pltpu.make_async_remote_copy(
            src_ref=src, dst_ref=dst, send_sem=send, recv_sem=recv, device_id=target, device_id_type=MESH
        )

    def strip_copy(i):
        part = strip.at[pl.ds(i * strip_rows, strip_rows)]
        return remote(part, part, strip_send.at[i], strip_recv.at[i], {"col": col + 1})

    def band_next(i):
        part = band.at[pl.ds(i * band_rows, band_rows)]
        return remote(part, part, band_send.at[i], band_recv.at[i], {"row": row + 2})

    def band_other(i):
        part = band.at[pl.ds(i * band_rows, band_rows)]
        return remote(part, part, band_pair.at[i], band_recv.at[i], {"row": row + 1})

    def piv_part(ref, i):
        return ref.at[pl.ds(i * piv_rows, piv_rows)]

    def piv_next(source, i):
        return remote(
            piv_part(source, i), piv_part(pivot, i), piv_send.at[i], piv_recv.at[i], {"row": row + 2}
        )

    def piv_other(source, i):
        return remote(
            piv_part(source, i), piv_part(pivot, i), piv_pair.at[i], piv_recv.at[i], {"row": row + 1}
        )

    n_strip = height // strip_rows
    n_band = PIV // band_rows
    n_piv = PIV // piv_rows
    for i in range(max(n_strip, n_band)):
        if i < n_strip:
            @pl.when(col > 0)
            def _():
                strip_copy(i).wait_recv()

            @pl.when(col < n_col - 1)
            def _():
                strip_copy(i).start()

        if i < n_piv:
            @pl.when(row > 0)
            def _():
                piv_next(pivot, i).wait_recv()

            for first, source in ((True, strip), (False, pivot)):
                here = (row == 0) if first else (row > 0)

                @pl.when(here & has_next)
                def _():
                    piv_next(source, i).start()

                @pl.when(here & even)
                def _():
                    piv_other(source, i).start()

        if i < n_band:
            @pl.when(row > 0)
            def _():
                band_next(i).wait_recv()

            @pl.when(has_next)
            def _():
                band_next(i).start()

            @pl.when(even)
            def _():
                band_other(i).start()

    for i in range(n_strip):
        @pl.when(col < n_col - 1)
        def _():
            strip_copy(i).wait_send()

    for i in range(n_band):
        @pl.when(has_next)
        def _():
            band_next(i).wait_send()

        @pl.when(even)
        def _():
            band_other(i).wait_send()

    for i in range(n_piv):
        @pl.when(has_next)
        def _():
            piv_next(pivot, i).wait_send()

        @pl.when(even)
        def _():
            piv_other(pivot, i).wait_send()


def spread_panels(strip, band, n_row, n_col):
    height = strip.shape[0]
    n_strip = height // BLK
    n_band = 2 * PIV // BLK
    n_piv = PIV // BLK
    dma = pltpu.SemaphoreType.DMA
    return pl.pallas_call(
        functools.partial(spread_kernel, n_row, n_col),
        out_shape=(
            jax.ShapeDtypeStruct(strip.shape, jnp.float32),
            jax.ShapeDtypeStruct(band.shape, jnp.float32),
            jax.ShapeDtypeStruct((PIV, PIV), jnp.float32),
        ),
        in_specs=[pl.BlockSpec(memory_space=pl.ANY)] * 2,
        out_specs=[pl.BlockSpec(memory_space=pl.ANY)] * 3,
        scratch_shapes=[
            dma((n_strip,)), dma((n_strip,)),
            dma((n_band,)), dma((n_band,)), dma((n_band,)),
            dma((n_piv,)), dma((n_piv,)), dma((n_piv,)),
        ],
        input_output_aliases={0: 0, 1: 1},
        compiler_params=pltpu.CompilerParams(collective_id=0, has_side_effects=True),
        name="spread_panels",
    )(strip, band)


def invert_pivots(pivot_block, pivots):
    identity = jnp.eye(pivot_block.shape[0], dtype=jnp.float32)
    masked = pivot_block * pivots[:, None] * pivots[None, :] + identity * (1.0 - pivots)[None, :]
    diagonal = jnp.sum(masked * identity, axis=1)
    approx = identity / diagonal[:, None]
    for iteration in range(6):
        product = jnp.dot(approx, masked, precision=HIGHEST)
        approx = jnp.dot(2.0 * identity - product, approx, precision=HIGHEST)
    return approx


def split(value):
    high = value.astype(jnp.bfloat16)
    low = (value - high.astype(jnp.float32)).astype(jnp.bfloat16)
    return high, low


def three_pass(left, high, low):
    left_high, left_low = split(left)
    total = jnp.dot(left_high, high, preferred_element_type=jnp.float32)
    total += jnp.dot(left_low, high, preferred_element_type=jnp.float32)
    return total + jnp.dot(left_high, low, preferred_element_type=jnp.float32)


def quarter_kernel(kept, a_ref, c_ref, high_ref, low_ref, out_ref):
    step = pl.program_id(0)
    tile = a_ref.shape[0]
    blocks = tile // (2 * BLK)
    left = jnp.concatenate(
        [c_ref[(2 * b + 1) * BLK:(2 * b + 2) * BLK, :] for b in range(blocks)], axis=0
    )
    total = three_pass(left, high_ref[...], low_ref[...])
    for b in range(blocks):
        for j in range(out_ref.shape[1] // BLK):
            keep = kept[step * 2 * blocks + 2 * b + 1, 2 * j + 1] != 0
            here = a_ref[(2 * b + 1) * BLK:(2 * b + 2) * BLK, (2 * j + 1) * BLK:(2 * j + 2) * BLK]
            out_ref[b * BLK:(b + 1) * BLK, j * BLK:(j + 1) * BLK] = (
                jnp.where(keep, here, 0.0)
                - total[b * BLK:(b + 1) * BLK, j * BLK:(j + 1) * BLK]
            )


def quarter_product(kept, matrix, left, high, low):
    height, breadth = matrix.shape
    tile = 4 * BLK
    half = breadth // 2
    return pl.pallas_call(
        quarter_kernel,
        grid=(height // tile,),
        out_shape=jax.ShapeDtypeStruct((height // 2, half), jnp.float32),
        in_specs=[
            pl.BlockSpec(memory_space=pltpu.SMEM),
            pl.BlockSpec((tile, breadth), lambda i: (i, 0)),
            pl.BlockSpec((tile, PIV), lambda i: (i, 0)),
            pl.BlockSpec((PIV, half), lambda i: (0, 0)),
            pl.BlockSpec((PIV, half), lambda i: (0, 0)),
        ],
        out_specs=pl.BlockSpec((tile // 2, half), lambda i: (i, 0)),
        compiler_params=pltpu.CompilerParams(vmem_limit_bytes=48 * 1024 * 1024),
        cost_estimate=pl.CostEstimate(
            flops=6 * height * breadth * PIV // 4, bytes_accessed=6 * height * breadth, transcendentals=0
        ),
        name="quarter_product",
    )(kept, matrix, left, high, low)


def full_kernel(kept, a_ref, c_ref, high_ref, low_ref, out_ref):
    step = pl.program_id(0)
    tile, breadth = a_ref.shape
    width = 4 * BLK
    left = c_ref[...]
    for start in range(0, breadth, width):
        total = three_pass(left, high_ref[:, start:start + width], low_ref[:, start:start + width])
        for b in range(tile // BLK):
            for j in range(width // BLK):
                rows = slice(b * BLK, (b + 1) * BLK)
                cols = slice(start + j * BLK, start + (j + 1) * BLK)
                keep = kept[step * (tile // BLK) + b, start // BLK + j] != 0
                out_ref[rows, cols] = (
                    jnp.where(keep, a_ref[rows, cols], 0.0) - total[rows, j * BLK:(j + 1) * BLK]
                )


def full_product(kept, matrix, left, high, low):
    height, breadth = matrix.shape
    tile = 2 * BLK
    return pl.pallas_call(
        full_kernel,
        grid=(height // tile,),
        out_shape=jax.ShapeDtypeStruct((height, breadth), jnp.float32),
        in_specs=[
            pl.BlockSpec(memory_space=pltpu.SMEM),
            pl.BlockSpec((tile, breadth), lambda i: (i, 0)),
            pl.BlockSpec((tile, PIV), lambda i: (i, 0)),
            pl.BlockSpec((PIV, breadth), lambda i: (0, 0)),
            pl.BlockSpec((PIV, breadth), lambda i: (0, 0)),
        ],
        out_specs=pl.BlockSpec((tile, breadth), lambda i: (i, 0)),
        compiler_params=pltpu.CompilerParams(vmem_limit_bytes=48 * 1024 * 1024),
        cost_estimate=pl.CostEstimate(
            flops=6 * height * breadth * PIV, bytes_accessed=11 * height * breadth, transcendentals=0
        ),
        name="full_product",
    )(kept, matrix, left, high, low)


def local(n_row, n_col, n_depth, front_matrix, block_mask, supernode_width):
    matrix = front_matrix[0]
    height, breadth = matrix.shape
    row_index = lax.axis_index("row")
    col_index = lax.axis_index("col")
    per_row = height // BLK
    per_col = breadth // BLK
    block_rows = row_index * per_row + jnp.arange(per_row)
    block_cols = col_index * per_col + jnp.arange(per_col)
    kept = (block_mask[0] != 0) | (block_rows[:, None] == block_cols[None, :])

    if PIV <= height and PIV <= breadth and n_row % 2 == 0:
        strip = masked_window(kept.astype(jnp.int32), matrix, height, PIV)
        band = masked_window(kept.astype(jnp.int32), matrix, PIV, breadth)
        strip, band, pivot = spread_panels(strip, band, n_row, n_col)
        pivot = jnp.where(row_index == 0, strip[:PIV], pivot)
    else:
        masked = expand_blocks(matrix, kept)
        strips, bands, pivot_parts = [], [], []
        for k in range(NSN):
            root, offset = divmod(k * SN, breadth)
            strips.append(from_root(masked[:, offset:offset + SN], "col", root))
        strip = jnp.concatenate(strips, axis=1)
        for k in range(NSN):
            root, offset = divmod(k * SN, height)
            bands.append(from_root(masked[offset:offset + SN, :], "row", root))
            pivot_parts.append(from_root(strip[offset:offset + SN, :], "row", root))
        band = jnp.concatenate(bands, axis=0)
        pivot = jnp.concatenate(pivot_parts, axis=0)

    global_rows = row_index * height + jnp.arange(height)
    global_cols = col_index * breadth + jnp.arange(breadth)
    live_rows = jnp.ones((height,), bool)
    live_cols = jnp.ones((breadth,), bool)
    blocks = {
        (i, j): pivot[i * SN:(i + 1) * SN, j * SN:(j + 1) * SN] for i in range(NSN) for j in range(NSN)
    }
    cols = [strip[:, k * SN:(k + 1) * SN] for k in range(NSN)]
    rows = [band[k * SN:(k + 1) * SN, :] for k in range(NSN)]
    left, right = [], []
    for k in range(NSN):
        start = k * SN
        width = supernode_width[0, k]
        pivots = (jnp.arange(SN) < width).astype(jnp.float32)
        live_rows &= (global_rows < start) | (global_rows >= start + width)
        live_cols &= (global_cols < start) | (global_cols >= start + width)
        inverse = invert_pivots(blocks[k, k], pivots) * pivots[None, :]
        for later in range(k):
            cols[k] = cols[k] - jnp.dot(left[later], blocks["solved", later, k], precision=HIGHEST)
            rows[k] = rows[k] - jnp.dot(blocks["panel", k, later], right[later], precision=HIGHEST)
        left.append(jnp.where(live_rows[:, None], cols[k] * pivots[None, :], 0.0))
        right.append(jnp.where(live_cols[None, :], jnp.dot(inverse, rows[k], precision=HIGHEST), 0.0))
        for i in range(k + 1, NSN):
            blocks["panel", i, k] = blocks[i, k] * pivots[None, :]
            blocks["solved", k, i] = jnp.dot(inverse, blocks[k, i], precision=HIGHEST)
        for i in range(k + 1, NSN):
            for j in range(k + 1, NSN):
                blocks[i, j] = blocks[i, j] - jnp.dot(
                    blocks["panel", i, k], blocks["solved", k, j], precision=HIGHEST
                )
    left = jnp.concatenate(left, axis=1)
    high, low = split(jnp.concatenate(right, axis=0))
    kept = kept.astype(jnp.int32)

    def odd_cols(value):
        return value.reshape(PIV, per_col // 2, 2, BLK)[:, :, 1, :].reshape(PIV, breadth // 2)

    quarter = quarter_product(kept, matrix, left, odd_cols(high), odd_cols(low))
    if n_depth == 2:
        depth_index = lax.axis_index("depth")
        part = breadth // 4
        away = lax.dynamic_slice_in_dim(quarter, (1 - depth_index) * part, part, axis=1)
        home = lax.dynamic_slice_in_dim(quarter, depth_index * part, part, axis=1)
        ancestor = home + lax.ppermute(away, "depth", [(0, 1), (1, 0)])
    else:
        ancestor = lax.psum_scatter(quarter, "depth", scatter_dimension=1, tiled=True)
    schur = full_product(kept, matrix, left, high, low)
    return (schur[None], ancestor)


def solution(mesh):
    placed = (P("depth", "row", "col"), P("depth", "row", "col"), P("depth", None))
    sizes = (mesh.shape["row"], mesh.shape["col"], mesh.shape["depth"])
    return jax.shard_map(
        functools.partial(local, *sizes),
        mesh=mesh,
        in_specs=placed,
        out_specs=(P("depth", "row", "col"), P("row", ("col", "depth"))),
        check_vma=False,
    )
```

```python
import functools

import jax
import jax.numpy as jnp
from jax import lax
from jax.experimental import pallas as pl
from jax.experimental.pallas import tpu as pltpu
from jax.sharding import PartitionSpec as P

SN = 256
BLK = 128
NSN = 3
PIV = SN * NSN
HIGHEST = lax.Precision.HIGHEST
MESH = pl.DeviceIdType.MESH


def from_root(value, axis, source):
    kept = jnp.where(lax.axis_index(axis) == source, value, 0).astype(value.dtype)
    return lax.psum(kept, axis)


def expand_blocks(matrix, kept_blocks):
    height, breadth = matrix.shape
    shaped = matrix.reshape(height // BLK, BLK, breadth // BLK, BLK)
    return jnp.where(kept_blocks[:, None, :, None], shaped, 0.0).reshape(height, breadth)


def masked_kernel(kept, a_ref, out_ref):
    step = pl.program_id(0)
    rows, cols = a_ref.shape
    for b in range(rows // BLK):
        for j in range(cols // BLK):
            keep = kept[step * (rows // BLK) + b, j] != 0
            here = (slice(b * BLK, (b + 1) * BLK), slice(j * BLK, (j + 1) * BLK))
            out_ref[here] = jnp.where(keep, a_ref[here], 0.0)


def masked_window(kept, matrix, rows, cols):
    tile = 2 * BLK
    return pl.pallas_call(
        masked_kernel,
        grid=(rows // tile,),
        out_shape=jax.ShapeDtypeStruct((rows, cols), jnp.float32),
        in_specs=[
            pl.BlockSpec(memory_space=pltpu.SMEM),
            pl.BlockSpec((tile, cols), lambda i: (i, 0)),
        ],
        out_specs=pl.BlockSpec((tile, cols), lambda i: (i, 0)),
        compiler_params=pltpu.CompilerParams(vmem_limit_bytes=32 * 1024 * 1024),
        name="masked_window",
    )(kept, matrix)


def spread_kernel(n_row, n_col, strip_in, band_in, strip, band, pivot, *sems):
    (strip_send, strip_recv, band_send, band_pair, band_recv, piv_send, piv_pair, piv_recv) = sems
    del strip_in, band_in
    row = lax.axis_index("row")
    col = lax.axis_index("col")
    even = lax.rem(row, 2) == 0
    has_next = even & (row + 2 < n_row)
    height = strip.shape[0]
    strip_rows = BLK // 2
    band_rows = BLK // 2
    piv_rows = BLK

    barrier = pltpu.get_barrier_semaphore()

    def greet(when, target):
        @pl.when(when)
        def _():
            pl.semaphore_signal(barrier, inc=1, device_id=target, device_id_type=MESH)

    greet(col > 0, {"col": col - 1})
    greet(col < n_col - 1, {"col": col + 1})
    greet(even, {"row": row + 1})
    greet(jnp.logical_not(even), {"row": row - 1})
    greet(has_next, {"row": row + 2})
    greet(even & (row >= 2), {"row": row - 2})

    peers = (col > 0).astype(jnp.int32) + (col < n_col - 1).astype(jnp.int32) + 1
    peers += has_next.astype(jnp.int32) + (even & (row >= 2)).astype(jnp.int32)
    pl.semaphore_wait(barrier, peers)

    def remote(src, dst, send, recv, target):
        return pltpu.make_async_remote_copy(
            src_ref=src, dst_ref=dst, send_sem=send, recv_sem=recv, device_id=target, device_id_type=MESH
        )

    def strip_copy(i):
        part = strip.at[pl.ds(i * strip_rows, strip_rows)]
        return remote(part, part, strip_send.at[i], strip_recv.at[i], {"col": col + 1})

    def band_next(i):
        part = band.at[pl.ds(i * band_rows, band_rows)]
        return remote(part, part, band_send.at[i], band_recv.at[i], {"row": row + 2})

    def band_other(i):
        part = band.at[pl.ds(i * band_rows, band_rows)]
        return remote(part, part, band_pair.at[i], band_recv.at[i], {"row": row + 1})

    def piv_part(ref, i):
        return ref.at[pl.ds(i * piv_rows, piv_rows)]

    def piv_next(source, i):
        return remote(
            piv_part(source, i), piv_part(pivot, i), piv_send.at[i], piv_recv.at[i], {"row": row + 2}
        )

    def piv_other(source, i):
        return remote(
            piv_part(source, i), piv_part(pivot, i), piv_pair.at[i], piv_recv.at[i], {"row": row + 1}
        )

    n_strip = height // strip_rows
    n_band = PIV // band_rows
    n_piv = PIV // piv_rows
    per_piv = piv_rows // strip_rows

    for i in range(n_strip):
        @pl.when(col == 0)
        def _():
            strip_copy(i).start()

    for i in range(n_band):
        @pl.when((row == 0) & has_next)
        def _():
            band_next(i).start()

        @pl.when(row == 0)
        def _():
            band_other(i).start()

    for step in range(max(n_strip, 2 * n_band + 2, 4 * n_piv + 7)):
        if step < n_strip:
            @pl.when(col > 0)
            def _():
                strip_copy(step).wait_recv()

            @pl.when((col > 0) & (col < n_col - 1))
            def _():
                strip_copy(step).start()

        if step % per_piv == per_piv - 1 and step // per_piv < n_piv:
            i = step // per_piv

            @pl.when((row == 0) & has_next)
            def _():
                piv_next(strip, i).start()

            @pl.when(row == 0)
            def _():
                piv_other(strip, i).start()

        if step >= 6 and (step - 6) % 4 == 0 and (step - 6) // 4 < n_piv:
            i = (step - 6) // 4

            @pl.when(row > 0)
            def _():
                piv_next(pivot, i).wait_recv()

            @pl.when((row > 0) & has_next)
            def _():
                piv_next(pivot, i).start()

            @pl.when((row > 0) & even)
            def _():
                piv_other(pivot, i).start()

        if step >= 2 and step % 2 == 0 and (step - 2) // 2 < n_band:
            i = (step - 2) // 2

            @pl.when(row > 0)
            def _():
                band_next(i).wait_recv()

            @pl.when((row > 0) & has_next)
            def _():
                band_next(i).start()

            @pl.when((row > 0) & even)
            def _():
                band_other(i).start()

    for i in range(n_strip):
        @pl.when(col < n_col - 1)
        def _():
            strip_copy(i).wait_send()

    for i in range(n_band):
        @pl.when(has_next)
        def _():
            band_next(i).wait_send()

        @pl.when(even)
        def _():
            band_other(i).wait_send()

    for i in range(n_piv):
        @pl.when(has_next)
        def _():
            piv_next(pivot, i).wait_send()

        @pl.when(even)
        def _():
            piv_other(pivot, i).wait_send()


def spread_panels(strip, band, n_row, n_col):
    height = strip.shape[0]
    n_strip = 2 * height // BLK
    n_band = 2 * PIV // BLK
    n_piv = PIV // BLK
    dma = pltpu.SemaphoreType.DMA
    return pl.pallas_call(
        functools.partial(spread_kernel, n_row, n_col),
        out_shape=(
            jax.ShapeDtypeStruct(strip.shape, jnp.float32),
            jax.ShapeDtypeStruct(band.shape, jnp.float32),
            jax.ShapeDtypeStruct((PIV, PIV), jnp.float32),
        ),
        in_specs=[pl.BlockSpec(memory_space=pl.ANY)] * 2,
        out_specs=[pl.BlockSpec(memory_space=pl.ANY)] * 3,
        scratch_shapes=[
            dma((n_strip,)), dma((n_strip,)),
            dma((n_band,)), dma((n_band,)), dma((n_band,)),
            dma((n_piv,)), dma((n_piv,)), dma((n_piv,)),
        ],
        input_output_aliases={0: 0, 1: 1},
        compiler_params=pltpu.CompilerParams(collective_id=0, has_side_effects=True),
        name="spread_panels",
    )(strip, band)


def invert_pivots(pivot_block, pivots):
    identity = jnp.eye(pivot_block.shape[0], dtype=jnp.float32)
    masked = pivot_block * pivots[:, None] * pivots[None, :] + identity * (1.0 - pivots)[None, :]
    diagonal = jnp.sum(masked * identity, axis=1)
    approx = identity / diagonal[:, None]
    for iteration in range(6):
        product = jnp.dot(approx, masked, precision=HIGHEST)
        approx = jnp.dot(2.0 * identity - product, approx, precision=HIGHEST)
    return approx


def split(value):
    high = lax.reduce_precision(value, 8, 7).astype(jnp.bfloat16)
    low = (value - high.astype(jnp.float32)).astype(jnp.bfloat16)
    return high, low


def three_pass(left, high, low):
    left_high = left.astype(jnp.bfloat16)
    left_low = (left - left_high.astype(jnp.float32)).astype(jnp.bfloat16)
    total = jnp.dot(left_high, high, preferred_element_type=jnp.float32)
    total += jnp.dot(left_low, high, preferred_element_type=jnp.float32)
    return total + jnp.dot(left_high, low, preferred_element_type=jnp.float32)


def odd_parts(ref, axis):
    parts = []
    for b in range(ref.shape[axis] // (2 * BLK)):
        where = slice((2 * b + 1) * BLK, (2 * b + 2) * BLK)
        parts.append(ref[where, :] if axis == 0 else ref[:, where])
    return jnp.concatenate(parts, axis=axis)


def away_kernel(side, kept, a_ref, c_ref, high_ref, low_ref, out_ref):
    step = pl.program_id(0)
    tile, breadth = a_ref.shape
    blocks = tile // (2 * BLK)
    total = three_pass(odd_parts(c_ref, 0), odd_parts(high_ref, 1), odd_parts(low_ref, 1))
    for b in range(blocks):
        for j in range(breadth // (2 * BLK)):
            keep = kept[step * 2 * blocks + 2 * b + 1, side[0] * (breadth // BLK) + 2 * j + 1] != 0
            here = a_ref[(2 * b + 1) * BLK:(2 * b + 2) * BLK, (2 * j + 1) * BLK:(2 * j + 2) * BLK]
            to = (slice(b * BLK, (b + 1) * BLK), slice(j * BLK, (j + 1) * BLK))
            out_ref[to] = jnp.where(keep, here, 0.0) - total[to]


def away_product(side, kept, matrix, left, high, low):
    height, breadth = matrix.shape
    tile = 4 * BLK
    half = breadth // 2
    return pl.pallas_call(
        away_kernel,
        out_shape=jax.ShapeDtypeStruct((height // 2, half // 2), jnp.float32),
        grid_spec=pltpu.PrefetchScalarGridSpec(
            num_scalar_prefetch=2,
            grid=(height // tile,),
            in_specs=[
                pl.BlockSpec((tile, half), lambda i, side, kept: (i, side[0])),
                pl.BlockSpec((tile, PIV), lambda i, side, kept: (i, 0)),
                pl.BlockSpec((PIV, half), lambda i, side, kept: (0, side[0])),
                pl.BlockSpec((PIV, half), lambda i, side, kept: (0, side[0])),
            ],
            out_specs=pl.BlockSpec((tile // 2, half // 2), lambda i, side, kept: (i, 0)),
        ),
        compiler_params=pltpu.CompilerParams(vmem_limit_bytes=48 * 1024 * 1024),
        cost_estimate=pl.CostEstimate(
            flops=6 * height * breadth * PIV // 8, bytes_accessed=6 * height * breadth, transcendentals=0
        ),
        name="away_product",
    )(side, kept, matrix, left, high, low)


def home_kernel(side, schur_ref, other_ref, out_ref):
    del side
    tile, breadth = schur_ref.shape
    for b in range(tile // (2 * BLK)):
        for j in range(breadth // (2 * BLK)):
            here = schur_ref[(2 * b + 1) * BLK:(2 * b + 2) * BLK, (2 * j + 1) * BLK:(2 * j + 2) * BLK]
            to = (slice(b * BLK, (b + 1) * BLK), slice(j * BLK, (j + 1) * BLK))
            out_ref[to] = here + other_ref[to]


def home_sum(side, schur, other):
    height, breadth = schur.shape
    tile = 4 * BLK
    half = breadth // 2
    return pl.pallas_call(
        home_kernel,
        out_shape=jax.ShapeDtypeStruct(other.shape, jnp.float32),
        grid_spec=pltpu.PrefetchScalarGridSpec(
            num_scalar_prefetch=1,
            grid=(height // tile,),
            in_specs=[
                pl.BlockSpec((tile, half), lambda i, side: (i, side[0])),
                pl.BlockSpec((tile // 2, half // 2), lambda i, side: (i, 0)),
            ],
            out_specs=pl.BlockSpec((tile // 2, half // 2), lambda i, side: (i, 0)),
        ),
        compiler_params=pltpu.CompilerParams(vmem_limit_bytes=48 * 1024 * 1024),
        name="home_sum",
    )(side, schur, other)


def full_kernel(kept, a_ref, c_ref, high_ref, low_ref, out_ref):
    step = pl.program_id(0)
    tile, breadth = a_ref.shape
    width = 4 * BLK
    left = c_ref[...]
    for start in range(0, breadth, width):
        total = three_pass(left, high_ref[:, start:start + width], low_ref[:, start:start + width])
        for b in range(tile // BLK):
            for j in range(width // BLK):
                rows = slice(b * BLK, (b + 1) * BLK)
                cols = slice(start + j * BLK, start + (j + 1) * BLK)
                keep = kept[step * (tile // BLK) + b, start // BLK + j] != 0
                out_ref[rows, cols] = (
                    jnp.where(keep, a_ref[rows, cols], 0.0) - total[rows, j * BLK:(j + 1) * BLK]
                )


def full_product(kept, matrix, left, high, low):
    height, breadth = matrix.shape
    tile = 2 * BLK
    return pl.pallas_call(
        full_kernel,
        grid=(height // tile,),
        out_shape=jax.ShapeDtypeStruct((height, breadth), jnp.float32),
        in_specs=[
            pl.BlockSpec(memory_space=pltpu.SMEM),
            pl.BlockSpec((tile, breadth), lambda i: (i, 0)),
            pl.BlockSpec((tile, PIV), lambda i: (i, 0)),
            pl.BlockSpec((PIV, breadth), lambda i: (0, 0)),
            pl.BlockSpec((PIV, breadth), lambda i: (0, 0)),
        ],
        out_specs=pl.BlockSpec((tile, breadth), lambda i: (i, 0)),
        compiler_params=pltpu.CompilerParams(vmem_limit_bytes=48 * 1024 * 1024),
        cost_estimate=pl.CostEstimate(
            flops=6 * height * breadth * PIV, bytes_accessed=11 * height * breadth, transcendentals=0
        ),
        name="full_product",
    )(kept, matrix, left, high, low)


def local(n_row, n_col, n_depth, front_matrix, block_mask, supernode_width):
    matrix = front_matrix[0]
    height, breadth = matrix.shape
    row_index = lax.axis_index("row")
    col_index = lax.axis_index("col")
    per_row = height // BLK
    per_col = breadth // BLK
    block_rows = row_index * per_row + jnp.arange(per_row)
    block_cols = col_index * per_col + jnp.arange(per_col)
    kept = (block_mask[0] != 0) | (block_rows[:, None] == block_cols[None, :])

    if PIV <= height and PIV <= breadth and n_row % 2 == 0:
        strip = masked_window(kept.astype(jnp.int32), matrix, height, PIV)
        band = masked_window(kept.astype(jnp.int32), matrix, PIV, breadth)
        strip, band, pivot = spread_panels(strip, band, n_row, n_col)
        pivot = jnp.where(row_index == 0, strip[:PIV], pivot)
    else:
        masked = expand_blocks(matrix, kept)
        strips, bands, pivot_parts = [], [], []
        for k in range(NSN):
            root, offset = divmod(k * SN, breadth)
            strips.append(from_root(masked[:, offset:offset + SN], "col", root))
        strip = jnp.concatenate(strips, axis=1)
        for k in range(NSN):
            root, offset = divmod(k * SN, height)
            bands.append(from_root(masked[offset:offset + SN, :], "row", root))
            pivot_parts.append(from_root(strip[offset:offset + SN, :], "row", root))
        band = jnp.concatenate(bands, axis=0)
        pivot = jnp.concatenate(pivot_parts, axis=0)

    global_rows = row_index * height + jnp.arange(height)
    global_cols = col_index * breadth + jnp.arange(breadth)
    live_rows = jnp.ones((height,), bool)
    live_cols = jnp.ones((breadth,), bool)
    blocks = {
        (i, j): pivot[i * SN:(i + 1) * SN, j * SN:(j + 1) * SN] for i in range(NSN) for j in range(NSN)
    }
    cols = [strip[:, k * SN:(k + 1) * SN] for k in range(NSN)]
    rows = [band[k * SN:(k + 1) * SN, :] for k in range(NSN)]
    left, right = [], []
    for k in range(NSN):
        start = k * SN
        width = supernode_width[0, k]
        pivots = (jnp.arange(SN) < width).astype(jnp.float32)
        live_rows &= (global_rows < start) | (global_rows >= start + width)
        live_cols &= (global_cols < start) | (global_cols >= start + width)
        inverse = invert_pivots(blocks[k, k], pivots) * pivots[None, :]
        for later in range(k):
            cols[k] = cols[k] - jnp.dot(left[later], blocks["solved", later, k], precision=HIGHEST)
            rows[k] = rows[k] - jnp.dot(blocks["panel", k, later], right[later], precision=HIGHEST)
        left.append(jnp.where(live_rows[:, None], cols[k] * pivots[None, :], 0.0))
        right.append(jnp.where(live_cols[None, :], jnp.dot(inverse, rows[k], precision=HIGHEST), 0.0))
        for i in range(k + 1, NSN):
            blocks["panel", i, k] = blocks[i, k] * pivots[None, :]
            blocks["solved", k, i] = jnp.dot(inverse, blocks[k, i], precision=HIGHEST)
        for i in range(k + 1, NSN):
            for j in range(k + 1, NSN):
                blocks[i, j] = blocks[i, j] - jnp.dot(
                    blocks["panel", i, k], blocks["solved", k, j], precision=HIGHEST
                )
    left = jnp.concatenate(left, axis=1)
    highs, lows = zip(*[split(value) for value in right])
    high, low = jnp.concatenate(highs, axis=0), jnp.concatenate(lows, axis=0)
    kept = kept.astype(jnp.int32)
    if n_depth == 2:
        side = lax.axis_index("depth").astype(jnp.int32).reshape(1)
        away = away_product(1 - side, kept, matrix, left, high, low)
        other = lax.ppermute(away, "depth", [(0, 1), (1, 0)])
        schur = full_product(kept, matrix, left, high, low)
        ancestor = home_sum(side, schur, other)
    else:
        schur = full_product(kept, matrix, left, high, low)
        quarter = schur.reshape(per_row, BLK, per_col, BLK)[1::2, :, 1::2, :]
        quarter = quarter.reshape(height // 2, breadth // 2)
        ancestor = lax.psum_scatter(quarter, "depth", scatter_dimension=1, tiled=True)
    return (schur[None], ancestor)


def solution(mesh):
    placed = (P("depth", "row", "col"), P("depth", "row", "col"), P("depth", None))
    sizes = (mesh.shape["row"], mesh.shape["col"], mesh.shape["depth"])
    return jax.shard_map(
        functools.partial(local, *sizes),
        mesh=mesh,
        in_specs=placed,
        out_specs=(P("depth", "row", "col"), P("row", ("col", "depth"))),
        check_vma=False,
    )
```
